128 devices in a mesh: tok: 64 (over x, y, z), grp: 2 (over core).
Axes of the slice: x: 4, y: 4, z: 4, core: 2. Of those that a mesh axis runs over, the one named last changes fastest.
Arguments:
- tokens: bfloat16 [131072, 1536], P('tok', 'grp'), may hold values from -8 to 8
- slot_keys: bfloat16 [1536, 256], P('tok', 'grp'), may hold values from -2 to 2
- w_in: bfloat16 [2, 64, 1536, 1024], P('grp', 'tok'), may hold values from -0.3125 to 0.3125
- w_out: bfloat16 [2, 64, 1024, 1536], P('grp', 'tok'), may hold values from -0.1875 to 0.1875
- out_grad: bfloat16 [131072, 1536], P('tok', 'grp'), may hold values from -0.59765625 to 0.59765625
Outputs:
- layer_out: bfloat16 [131072, 1536], P('tok', 'grp')
- tokens_grad: bfloat16 [131072, 1536], P('tok', 'grp')
- keys_grad: float32 [1536, 256], P('tok', 'grp')
- w_in_grad: bfloat16 [2, 64, 1536, 1024], P('grp', 'tok')
- w_out_grad: bfloat16 [2, 64, 1024, 1536], P('grp', 'tok')
The draws below stay inside these ranges and needn't reach their ends.
All inputs are finite; a program needn't handle non-finite values.
Results may differ from the reference program's by a relative error of at most 0.02.
Values may be sent and summed in bfloat16 or wider, within the bound.
A program may use at most 192 MiB of HBM per device.

```python
import math
import jax
import jax.numpy as jnp
from jax import lax

D = 1536
HID = 1024
SLOTS_EXP = 2
GROUPS = 2
EXP_GRP = 64
EXPERTS = 128
SLOTS = 256
TOKENS = 131072


def draw_tokens(key, part):
    key = jax.random.fold_in(key, 3)
    values = jax.random.normal(key, (TOKENS, D), jnp.float32)
    return jnp.clip(values, -8.0, 8.0).astype(jnp.bfloat16)


def draw_slot_keys(key, part):
    key = jax.random.fold_in(key, 4)
    spread = 3.0 / math.sqrt(D)
    values = jax.random.normal(key, (D, SLOTS), jnp.float32) * spread
    return jnp.clip(values, -2.0, 2.0).astype(jnp.bfloat16)


def level_of(rng, shape, shards, low, high):
    loudness = 1.0
    for axis_at, shards_of in shards:
        heights = jax.random.uniform(jax.random.fold_in(jax.random.fold_in(rng, 6), axis_at), (shards_of,), jnp.float32, low / len(shards), high / len(shards))
        loudness = loudness * jnp.repeat(jnp.exp(heights), shape[axis_at] // shards_of).reshape((-1,) + (1,) * (len(shape) - 1 - axis_at))
    return loudness


def scatter_about(key, shape, scale, bound, cuts=(), held_as=jnp.bfloat16):
    entries = jax.random.normal(key, shape, jnp.float32) * scale
    if len(cuts) > 0:
        entries = level_of(key, shape, cuts, -0.22, 0.18) * entries
    return jnp.clip(entries, min=-bound, max=bound).astype(held_as)


def setup_inputs(seed: int = 0) -> dict:
    arg_keys = jax.random.split(jax.random.key(seed), 6)
    tokens = draw_tokens(jax.random.fold_in(arg_keys[5], 71), 0)
    slot_keys = draw_slot_keys(jax.random.fold_in(arg_keys[5], 71), 0)
    w_in = scatter_about(arg_keys[2], (GROUPS, EXP_GRP, D, HID), (D // 4) ** -0.5, 0.3125, ((0, 2), (1, 64)))
    w_out = scatter_about(arg_keys[3], (GROUPS, EXP_GRP, HID, D), HID ** -0.5, 0.1875, ((0, 2), (1, 64)))
    out_grad = scatter_about(arg_keys[4], (TOKENS, D), 0.1, 0.59765625, ((0, 64), (1, 2)))
    return {"tokens": tokens, "slot_keys": slot_keys, "w_in": w_in, "w_out": w_out, "out_grad": out_grad}


def gelu_exact(argument):
    return 0.5 * argument * (1.0 + jax.scipy.special.erf(argument / math.sqrt(2.0)))

def gelu_slope(argument):
    cumulative = 0.5 * (1.0 + jax.scipy.special.erf(argument / math.sqrt(2.0)))
    density = jnp.exp(-0.5 * argument * argument) / math.sqrt(2.0 * math.pi)
    return cumulative + argument * density

def contract_rows(former, latter):
    return lax.dot_general(former, latter, (((0,), (0,)), ((), ())), preferred_element_type=jnp.float32)

def contract_cols(former, latter):
    return lax.dot_general(former, latter, (((1,), (1,)), ((), ())), preferred_element_type=jnp.float32)

def expert_forward(operands):
    slot_rows, in_matrix, out_matrix = operands
    pre_act = jnp.dot(slot_rows, in_matrix, preferred_element_type=jnp.float32)
    hidden = gelu_exact(pre_act).astype(jnp.bfloat16)
    slot_out = jnp.dot(hidden, out_matrix, preferred_element_type=jnp.float32).astype(jnp.bfloat16)
    return (pre_act, hidden, slot_out)

def expert_backward(operands):
    slot_rows, pre_act, hidden, in_matrix, out_matrix, grad_rows = operands
    out_part = contract_rows(hidden, grad_rows).astype(jnp.bfloat16)
    hidden_grad = contract_cols(grad_rows, out_matrix)
    pre_grad = (hidden_grad * gelu_slope(pre_act)).astype(jnp.bfloat16)
    in_part = contract_rows(slot_rows, pre_grad).astype(jnp.bfloat16)
    slot_grad = contract_cols(pre_grad, in_matrix)
    return (in_part, out_part, slot_grad)

def reference(tokens, slot_keys, w_in, w_out, out_grad):
    logits = jnp.dot(tokens, slot_keys, preferred_element_type=jnp.float32)
    disp_peak = lax.optimization_barrier(jnp.max(logits, axis=0))
    disp_exp = jnp.exp(logits - disp_peak[None, :])
    disp_total = lax.optimization_barrier(jnp.sum(disp_exp, axis=0))
    disp_weight = disp_exp.astype(jnp.bfloat16)
    slot_in_f = contract_rows(disp_weight, tokens) / disp_total[:, None]
    slot_in = slot_in_f.astype(jnp.bfloat16)
    experts_in = slot_in.reshape(EXPERTS, SLOTS_EXP, D)
    in_stack = w_in.reshape(EXPERTS, D, HID)
    out_stack = w_out.reshape(EXPERTS, HID, D)
    pre_act, hidden, slot_out = lax.map(expert_forward, (experts_in, in_stack, out_stack))
    slot_flat = slot_out.reshape(SLOTS, D)
    comb_peak = lax.optimization_barrier(jnp.max(logits, axis=1))
    comb_exp = jnp.exp(logits - comb_peak[:, None])
    comb_total = lax.optimization_barrier(jnp.sum(comb_exp, axis=1))
    comb_weight = comb_exp.astype(jnp.bfloat16)
    layer_out = (jnp.dot(comb_weight, slot_flat, preferred_element_type=jnp.float32) / comb_total[:, None]).astype(jnp.bfloat16)
    scaled_grad = (out_grad / comb_total[:, None]).astype(jnp.bfloat16)
    out_slot_grad = contract_rows(comb_weight, scaled_grad).astype(jnp.bfloat16)
    grad_stack = out_slot_grad.reshape(EXPERTS, SLOTS_EXP, D)
    in_parts, out_parts, slot_grads = lax.map(expert_backward, (experts_in, pre_act, hidden, in_stack, out_stack, grad_stack))
    w_in_grad = in_parts.reshape(GROUPS, EXP_GRP, D, HID)
    w_out_grad = out_parts.reshape(GROUPS, EXP_GRP, HID, D)
    slot_in_grad = slot_grads.reshape(SLOTS, D)
    routed = (slot_in_grad / disp_total[:, None]).astype(jnp.bfloat16)
    out_dot = contract_cols(out_grad, slot_flat)
    mix_dot = lax.optimization_barrier(jnp.sum(comb_exp * out_dot, axis=1)) / comb_total
    in_dot = contract_cols(tokens, routed)
    disp_dot = lax.optimization_barrier(jnp.sum(disp_exp * in_dot, axis=0)) / disp_total
    logit_grad = (comb_exp / comb_total[:, None] * (out_dot - mix_dot[:, None]) + disp_exp * (in_dot - disp_dot[None, :])).astype(jnp.bfloat16)
    both_weight = jnp.concatenate([disp_weight, logit_grad], axis=1)
    both_values = jnp.concatenate([routed, slot_keys.T], axis=0)
    tokens_grad = jnp.dot(both_weight, both_values, preferred_element_type=jnp.float32).astype(jnp.bfloat16)
    keys_grad = contract_rows(tokens, logit_grad)
    return (layer_out, tokens_grad, keys_grad, w_in_grad, w_out_grad)
```

```python
import functools
import math

import jax
import jax.numpy as jnp
from jax import lax
from jax.experimental import pallas as pl
from jax.experimental.pallas import tpu as pltpu
from jax.sharding import PartitionSpec as P

MESH = pl.DeviceIdType.MESH
F32 = jnp.float32
BF16 = jnp.bfloat16

NT = 64
SIDE = 4
TOK = 2048
HALF = 768
WIDTH = 1536
HID = 1024
SLOTS = 256
SLOT_ROWS = 4
GROUPS6 = HALF // 128
DATA_ROWS = SLOT_ROWS * GROUPS6
MSG_ROWS = 32
CHUNK = 512
NCHUNK = TOK // CHUNK
KROWS = 24

CONTRACT_ROWS = (((0,), (0,)), ((), ()))
CONTRACT_COLS = (((1,), (1,)), ((), ()))


def dot_nn(a, b):
    return jnp.dot(a, b, preferred_element_type=F32)


def dot_tn(a, b):
    return lax.dot_general(a, b, CONTRACT_ROWS, preferred_element_type=F32)


def dot_nt(a, b):
    return lax.dot_general(a, b, CONTRACT_COLS, preferred_element_type=F32)


def gelu_parts(v):
    cumulative = 0.5 * (1.0 + lax.erf(v * (1.0 / math.sqrt(2.0))))
    density = jnp.exp(-0.5 * v * v) * (1.0 / math.sqrt(2.0 * math.pi))
    return v * cumulative, cumulative + v * density


def rows_at(c):
    return pl.ds(pl.multiple_of(c * CHUNK, CHUNK), CHUNK)


def split_hi_lo(value, shape):
    lane = lax.broadcasted_iota(jnp.int32, shape, 1)
    hi = value.astype(BF16).astype(F32)
    return jnp.where(lane < 64, hi, value - hi)


def join_hi_lo(value):
    return value + pltpu.roll(value, 64, 1)


def kernel(
    tokens, keys, w_in, w_out, grads,
    lay_out, tok_out, key_out, win_out, wout_out,
    x, dy, wi, wo, part, logit, comb, combw, dispw, lgs, lgr, lg, lay, tgr, wig, wog,
    acc, flat, keyf, keymsg, keyland, osgmsg, osgland, slotmsg, slotland, outmsg, outland,
    rtmsg, rtland, kgmsg, kgland, sval, rval, colmax, colsum,
    osgx, slotx, outx, outr, rtx, rtr, arow, grow, srow, prow,
    load_sem, out_sem, pair_s, pair_r, ls, lr, gs, gr, a2a_s, a2a_r,
):
    t = lax.axis_index("tok")
    g = lax.axis_index("grp")
    other = 1 - g
    cx, cy, cz = t // 16, lax.rem(t // 4, 4), lax.rem(t, 4)

    loads = [
        pltpu.make_async_copy(tokens, x, load_sem.at[0]),
        pltpu.make_async_copy(grads, dy, load_sem.at[1]),
        pltpu.make_async_copy(w_out.at[0, 0], wo, load_sem.at[2]),
        pltpu.make_async_copy(w_in.at[0, 0], wi, load_sem.at[3]),
    ]
    for copy in loads:
        copy.start()

    barrier = pltpu.get_barrier_semaphore()

    def greet(i, _):
        p = lax.rem(t + i, NT)
        pl.semaphore_signal(barrier, inc=1, device_id={"tok": p, "grp": g}, device_id_type=MESH)
        pl.semaphore_signal(barrier, inc=1, device_id={"tok": p, "grp": other}, device_id_type=MESH)
        return 0

    lax.fori_loop(1, NT, greet, 0)
    pl.semaphore_signal(barrier, inc=1, device_id={"tok": t, "grp": other}, device_id_type=MESH)

    row = lax.broadcasted_iota(jnp.int32, (128, 128), 0)
    col = lax.broadcasted_iota(jnp.int32, (128, 128), 1)
    order = jnp.where(row == 2 * lax.rem(col, 64) + col // 64, 1.0, 0.0).astype(BF16)
    keymsg[0:KROWS, :] = dot_nn(keys[...], order).astype(BF16)
    pl.semaphore_wait(barrier, 2 * NT - 1)

    def partner(i):
        a, b, c = i // 16, lax.rem(i // 4, 4), lax.rem(i, 4)
        px, py, pz = lax.rem(cx + 6 - a, 4), lax.rem(cy + 6 - b, 4), lax.rem(cz + 6 - c, 4)
        return px * 16 + py * 4 + pz

    def each_partner(send):
        def step(i, _):
            send(partner(i))
            return 0

        lax.fori_loop(0, 42, step, 0)
        lax.fori_loop(43, NT, step, 0)

    def pair_copy(i, src, dst):
        return pltpu.make_async_remote_copy(
            src, dst, pair_s.at[i], pair_r.at[i], device_id={"tok": t, "grp": other}, device_id_type=MESH
        )

    def landed(i, buffer):
        pltpu.make_async_copy(buffer, buffer, a2a_r.at[i]).wait()

    def sent(i, block):
        pltpu.make_async_copy(block, block, a2a_s.at[i]).wait()

    half = t // 32
    place = g * 32 + lax.rem(t, 32)

    def send_keys(p):
        pltpu.make_async_remote_copy(
            keymsg, keyland.at[place], a2a_s.at[0], a2a_r.at[0],
            device_id={"tok": p, "grp": half}, device_id_type=MESH,
        ).start()

    each_partner(send_keys)

    @pl.when(half == g)
    def _():
        pltpu.make_async_copy(keymsg, keyland.at[place], a2a_r.at[0]).start()

    @pl.when(half != g)
    def _():
        pltpu.make_async_remote_copy(
            keymsg, keyland.at[place], a2a_s.at[0], a2a_r.at[0],
            device_id={"tok": t, "grp": other}, device_id_type=MESH,
        ).start()

    landed(0, keyland)
    for h in range(2):
        block = keyland[h * 32:(h + 1) * 32, 0:KROWS, :].astype(F32)
        keyf[:, h * 128:(h + 1) * 128] = block.reshape(HALF, 128).astype(BF16)

    def logit_copy(c):
        return pltpu.make_async_remote_copy(
            part.at[rows_at(c)], logit.at[rows_at(c)], ls.at[c], lr.at[c],
            device_id={"tok": t, "grp": other}, device_id_type=MESH,
        )

    loads[0].wait()

    def logits_step(c, _):
        part[rows_at(c), :] = dot_nn(x[rows_at(c), :], keyf[...])
        logit_copy(c).start()
        return 0

    lax.fori_loop(0, NCHUNK, logits_step, 0)

    loads[1].wait()
    colmax[...] = jnp.full((8, SLOTS), -jnp.inf, F32)
    acc[...] = jnp.zeros((SLOTS, HALF), F32)

    def comb_step(c, _):
        rows = rows_at(c)
        logit_copy(c).wait_recv()
        values = logit[rows, :] + part[rows, :]
        logit[rows, :] = values
        colmax[...] = jnp.maximum(colmax[...], jnp.max(values.reshape(CHUNK // 8, 8, SLOTS), axis=0))
        weights = jnp.exp(values - jnp.max(values, axis=1, keepdims=True))
        weights = weights / jnp.sum(weights, axis=1, keepdims=True)
        comb[rows, :] = weights
        low = weights.astype(BF16)
        combw[rows, :] = low
        acc[...] += dot_tn(low, dy[rows, :])
        return 0

    lax.fori_loop(0, NCHUNK, comb_step, 0)

    def to_messages():
        for j in range(SLOT_ROWS):
            for q in range(GROUPS6):
                flat[pl.ds(4 * q + j, NT, stride=MSG_ROWS), :] = acc[64 * j:64 * (j + 1), 128 * q:128 * (q + 1)]

    def from_messages(dst):
        for j in range(SLOT_ROWS):
            for q in range(GROUPS6):
                dst[64 * j:64 * (j + 1), 128 * q:128 * (q + 1)] = (
                    flat[pl.ds(4 * q + j, NT, stride=MSG_ROWS), :].astype(BF16)
                )

    def to_lanes(r):
        column = jnp.concatenate(
            [flat[pl.ds(r + j, NT, stride=MSG_ROWS), :] for j in range(SLOT_ROWS)], axis=0
        )
        return column.T[0:1, :]

    def scatter(i, msg, land):
        def send(p):
            pltpu.make_async_remote_copy(
                msg.at[p], land.at[t], a2a_s.at[i], a2a_r.at[i],
                device_id={"tok": p, "grp": g}, device_id_type=MESH,
            ).start()

        each_partner(send)
        pltpu.make_async_copy(msg.at[t], land.at[t], a2a_r.at[i]).start()

    def spread(i, msg, land):
        def send(p):
            pltpu.make_async_remote_copy(
                msg, land.at[t], a2a_s.at[i], a2a_r.at[i],
                device_id={"tok": p, "grp": g}, device_id_type=MESH,
            ).start()

        each_partner(send)
        pltpu.make_async_copy(msg, land.at[t], a2a_r.at[i]).start()

    to_messages()
    osgmsg[...] = flat[...].reshape(NT, MSG_ROWS, 128).astype(BF16)
    scatter(1, osgmsg, osgland)

    peak = jnp.max(colmax[...], axis=0, keepdims=True).astype(BF16).astype(F32)
    acc[...] = jnp.zeros((SLOTS, HALF), F32)
    colsum[...] = jnp.zeros((8, SLOTS), F32)

    def disp_step(c, _):
        rows = rows_at(c)
        weights = jnp.exp(logit[rows, :] - peak)
        colsum[...] += jnp.sum(weights.reshape(CHUNK // 8, 8, SLOTS), axis=0)
        acc[...] += dot_tn(weights.astype(BF16), x[rows, :])
        return 0

    lax.fori_loop(0, NCHUNK, disp_step, 0)
    total = jnp.sum(colsum[...], axis=0, keepdims=True)
    peak_col = jnp.broadcast_to(peak, (128, SLOTS)).T
    total_col = split_hi_lo(jnp.broadcast_to(total, (128, SLOTS)).T, (SLOTS, 128))
    to_messages()
    for j in range(SLOT_ROWS):
        flat[pl.ds(DATA_ROWS + j, NT, stride=MSG_ROWS), :] = peak_col[64 * j:64 * (j + 1), :]
        flat[pl.ds(DATA_ROWS + 4 + j, NT, stride=MSG_ROWS), :] = total_col[64 * j:64 * (j + 1), :]
    slotmsg[...] = flat[...].reshape(NT, MSG_ROWS, 128).astype(BF16)
    scatter(2, slotmsg, slotland)

    row16 = lax.broadcasted_iota(jnp.int32, (16, 1), 0)
    mine = jnp.where(row16 // 2 == g, 1.0, 0.0).astype(F32)

    def to_rows(dst, src):
        dst[...] = jnp.zeros((16, WIDTH), F32)
        for h in range(2):
            for q in range(GROUPS6):
                at = (h * GROUPS6 + q) * 128
                dst[0:SLOT_ROWS, at:at + 128] = src[h, 4 * q:4 * q + 4, :]

    def from_rows(dst, value):
        for h in range(2):
            for q in range(GROUPS6):
                at = (h * GROUPS6 + q) * 128
                dst[h, 4 * q:4 * q + 4, :] = value[0:SLOT_ROWS, at:at + 128]

    landed(1, osgland)
    osgx[g, :, :] = jnp.sum(osgland[:, 0:DATA_ROWS, :].astype(F32), axis=0)
    osg_pair = pair_copy(0, osgx.at[g], osgx.at[g])
    osg_pair.start()
    osg_pair.wait_recv()
    to_rows(grow, osgx)
    out_grad = (grow[...] * mine).astype(BF16)
    loads[2].wait()
    hidden_grad = dot_nt(out_grad, wo[...])

    landed(2, slotland)
    stats = slotland[:, DATA_ROWS:MSG_ROWS, :].astype(F32)
    row8 = lax.broadcasted_iota(jnp.int32, (NT, 8, 128), 1)
    swapped = jnp.concatenate([stats[:, 4:8, :], stats[:, 0:4, :]], axis=1)
    peaks = jnp.where(row8 < 4, stats, swapped)
    totals = jnp.where(row8 < 4, swapped, stats)
    top = jnp.max(peaks, axis=0)
    scale = jnp.exp(peaks - top[None])
    whole = join_hi_lo(jnp.sum(scale * totals, axis=0))
    for q in range(DATA_ROWS // 8):
        block = slotland[:, 8 * q:8 * (q + 1), :].astype(F32)
        slotx[g, 8 * q:8 * (q + 1), :] = jnp.sum(block * scale, axis=0) / whole
    slot_pair = pair_copy(1, slotx.at[g], slotx.at[g])
    slot_pair.start()
    slot_pair.wait_recv()
    to_rows(srow, slotx)
    slot_in = srow[...].astype(BF16)
    loads[3].wait()
    pre_act = dot_nn(slot_in, wi[...])
    hidden, slope = gelu_parts(pre_act)
    hidden = hidden.astype(BF16)
    slot_out = dot_nn(hidden, wo[...]) * mine
    from_rows(outx, slot_out)
    out_pair = pair_copy(2, outx.at[other], outr)
    out_pair.start()
    out_pair.wait_recv()
    outmsg[0:DATA_ROWS, :] = (outx[g, :, :] + outr[...]).astype(BF16)
    spread(3, outmsg, outland)

    pre_grad = (hidden_grad * slope).astype(BF16)
    slot_in_grad = dot_nt(pre_grad, wi[...])
    arow[...] = jnp.zeros((16, 128), F32)
    arow[0:SLOT_ROWS, :] = whole[0:SLOT_ROWS, :]
    whole_rows = jnp.where(row16 < SLOT_ROWS, arow[...], 1.0)
    routed = slot_in_grad / jnp.concatenate([whole_rows] * (WIDTH // 128), axis=1)
    routed = routed.astype(BF16).astype(F32) * mine
    from_rows(rtx, routed)
    products = srow[...] * routed
    for h in range(2):
        share = jnp.sum(products[:, h * HALF:(h + 1) * HALF], axis=1, keepdims=True)
        share = jnp.broadcast_to(share, (16, 128))
        rtx[h, DATA_ROWS:DATA_ROWS + 4, :] = top[0:SLOT_ROWS, :] * mine[0:SLOT_ROWS, :]
        rtx[h, DATA_ROWS + 4:MSG_ROWS, :] = share[0:SLOT_ROWS, :]
    rt_pair = pair_copy(3, rtx.at[other], rtr)
    rt_pair.start()
    rt_pair.wait_recv()
    rtmsg[0:DATA_ROWS, :] = (rtx[g, 0:DATA_ROWS, :] + rtr[0:DATA_ROWS, :]).astype(BF16)
    tail = rtx[g, DATA_ROWS:MSG_ROWS, :] + rtr[DATA_ROWS:MSG_ROWS, :]
    lane8 = lax.broadcasted_iota(jnp.int32, (8, 128), 1)
    row8b = lax.broadcasted_iota(jnp.int32, (8, 128), 0)
    high = tail.astype(BF16).astype(F32)
    tail = jnp.where((row8b < 4) | (lane8 < 64), high, tail - high)
    rtmsg[DATA_ROWS:MSG_ROWS, :] = tail.astype(BF16)
    spread(4, rtmsg, rtland)

    wog[...] = dot_tn(hidden, out_grad).astype(BF16)
    wout_copy = pltpu.make_async_copy(wog, wout_out.at[0, 0], out_sem.at[0])
    wout_copy.start()
    wig[...] = dot_tn(slot_in, pre_grad).astype(BF16)
    win_copy = pltpu.make_async_copy(wig, win_out.at[0, 0], out_sem.at[1])
    win_copy.start()

    landed(3, outland)
    flat[...] = outland[...].astype(F32).reshape(NT * MSG_ROWS, 128)
    from_messages(sval)

    def out_step(c, _):
        rows = rows_at(c)
        lay[rows, :] = dot_nn(combw[rows, :], sval[...]).astype(BF16)
        pltpu.make_async_copy(lay.at[rows], lay_out.at[rows], out_sem.at[2]).start()
        weights = comb[rows, :]
        out_dot = dot_nt(dy[rows, :], sval[...])
        mix = jnp.sum(weights * out_dot, axis=1, keepdims=True)
        comb[rows, :] = weights * (out_dot - mix)
        return 0

    lax.fori_loop(0, NCHUNK, out_step, 0)

    landed(4, rtland)
    flat[...] = rtland[...].astype(F32).reshape(NT * MSG_ROWS, 128)
    from_messages(rval)
    top_row = to_lanes(DATA_ROWS)
    lane_sum = jnp.concatenate(
        [flat[pl.ds(DATA_ROWS + 4 + j, NT, stride=MSG_ROWS), :] for j in range(SLOT_ROWS)], axis=0
    )
    disp_dot = join_hi_lo(lane_sum).T[0:1, :]

    def grad_copy(c):
        return pltpu.make_async_remote_copy(
            lgs.at[rows_at(c)], lgr.at[rows_at(c)], gs.at[c], gr.at[c],
            device_id={"tok": t, "grp": other}, device_id_type=MESH,
        )

    def in_step(c, _):
        rows = rows_at(c)
        weights = jnp.exp(logit[rows, :] - top_row)
        dispw[rows, :] = weights.astype(BF16)
        in_dot = dot_nt(x[rows, :], rval[...])
        lgs[rows, :] = (comb[rows, :] + weights * (in_dot - disp_dot)).astype(BF16)
        grad_copy(c).start()
        return 0

    lax.fori_loop(0, NCHUNK, in_step, 0)
    acc[...] = jnp.zeros((SLOTS, HALF), F32)

    def keys_step(c, _):
        rows = rows_at(c)
        grad_copy(c).wait_recv()
        low = (lgs[rows, :].astype(F32) + lgr[rows, :].astype(F32)).astype(BF16)
        lg[rows, :] = low
        acc[...] += dot_tn(low, x[rows, :])
        return 0

    lax.fori_loop(0, NCHUNK, keys_step, 0)

    for h in range(2):
        for q in range(GROUPS6):
            turned = acc[h * 128:(h + 1) * 128, q * 128:(q + 1) * 128].T
            flat[h * HALF + q * 128:h * HALF + (q + 1) * 128, :] = turned
    kgmsg[:, 0:KROWS, :] = flat[0:2 * HALF, :].reshape(NT, KROWS, 128).astype(BF16)

    def key_target(i):
        a, b, c, d = i // 32, lax.rem(i // 8, 4), lax.rem(i // 2, 4), lax.rem(i, 2)
        py, pz = lax.rem(cy + 6 - b, 4), lax.rem(cz + 6 - c, 4)
        return a * 16 + py * 4 + pz, d

    def send_grad(i, _):
        p, d = key_target(i)

        @pl.when((g * 32 + p != t) | (d != g))
        def _():
            pltpu.make_async_remote_copy(
                kgmsg.at[d * 32 + p], kgland.at[t], a2a_s.at[5], a2a_r.at[5],
                device_id={"tok": g * 32 + p, "grp": d}, device_id_type=MESH,
            ).start()

        return 0

    lax.fori_loop(0, NT, send_grad, 0)

    @pl.when(half == g)
    def _():
        pltpu.make_async_copy(kgmsg.at[g * 32 + lax.rem(t, 32)], kgland.at[t], a2a_r.at[5]).start()

    def tok_step(c, _):
        rows = rows_at(c)
        value = dot_nn(dispw[rows, :], rval[...]) + dot_nt(lg[rows, :], keyf[...])
        tgr[rows, :] = value.astype(BF16)
        pltpu.make_async_copy(tgr.at[rows], tok_out.at[rows], out_sem.at[3]).start()
        return 0

    lax.fori_loop(0, NCHUNK, tok_step, 0)

    landed(5, kgland)
    key_out[...] = jnp.sum(kgland[:, 0:KROWS, :].astype(F32), axis=0)

    for pair in (osg_pair, slot_pair, out_pair, rt_pair):
        pair.wait_send()

    def drain(c, _):
        logit_copy(c).wait_send()
        grad_copy(c).wait_send()
        return 0

    lax.fori_loop(0, NCHUNK, drain, 0)
    sent(1, osgmsg.at[pl.ds(0, NT - 1)])
    sent(2, slotmsg.at[pl.ds(0, NT - 1)])
    sent(3, outland.at[pl.ds(0, NT - 1)])
    sent(4, rtland.at[pl.ds(0, NT - 1)])

    @pl.when(half == g)
    def _():
        sent(0, keyland.at[pl.ds(0, NT - 1)])
        sent(5, kgmsg.at[pl.ds(0, NT - 1)])

    @pl.when(half != g)
    def _():
        sent(0, keyland)
        sent(5, kgmsg)

    wout_copy.wait()
    win_copy.wait()
    pltpu.make_async_copy(lay, lay_out, out_sem.at[2]).wait()
    pltpu.make_async_copy(tgr, tok_out, out_sem.at[3]).wait()


def body(tokens, slot_keys, w_in, w_out, out_grad):
    anywhere = pl.BlockSpec(memory_space=pl.ANY)
    vmem = pl.BlockSpec(memory_space=pltpu.VMEM)
    buf = pltpu.VMEM
    dma = pltpu.SemaphoreType.DMA
    messages = buf((NT, MSG_ROWS, 128), BF16)
    layer_out, tokens_grad, keys_grad, w_in_grad, w_out_grad = pl.pallas_call(
        kernel,
        out_shape=(
            jax.ShapeDtypeStruct((TOK, HALF), BF16),
            jax.ShapeDtypeStruct((TOK, HALF), BF16),
            jax.ShapeDtypeStruct((KROWS, 128), F32),
            jax.ShapeDtypeStruct(w_in.shape, BF16),
            jax.ShapeDtypeStruct(w_out.shape, BF16),
        ),
        in_specs=[anywhere, vmem, anywhere, anywhere, anywhere],
        out_specs=[anywhere, anywhere, vmem, anywhere, anywhere],
        scratch_shapes=[
            buf((TOK, HALF), BF16),
            buf((TOK, HALF), BF16),
            buf((WIDTH, HID), BF16),
            buf((HID, WIDTH), BF16),
            buf((TOK, SLOTS), F32),
            buf((TOK, SLOTS), F32),
            buf((TOK, SLOTS), F32),
            buf((TOK, SLOTS), BF16),
            buf((TOK, SLOTS), BF16),
            buf((TOK, SLOTS), BF16),
            buf((TOK, SLOTS), BF16),
            buf((TOK, SLOTS), BF16),
            buf((TOK, HALF), BF16),
            buf((TOK, HALF), BF16),
            buf((WIDTH, HID), BF16),
            buf((HID, WIDTH), BF16),
            buf((SLOTS, HALF), F32),
            buf((NT * MSG_ROWS, 128), F32),
            buf((HALF, SLOTS), BF16),
            buf((MSG_ROWS, 128), BF16),
            messages,
            messages,
            messages,
            messages,
            messages,
            buf((MSG_ROWS, 128), BF16),
            messages,
            buf((MSG_ROWS, 128), BF16),
            messages,
            messages,
            messages,
            buf((SLOTS, HALF), BF16),
            buf((SLOTS, HALF), BF16),
            buf((8, SLOTS), F32),
            buf((8, SLOTS), F32),
            buf((2, DATA_ROWS, 128), F32),
            buf((2, DATA_ROWS, 128), F32),
            buf((2, DATA_ROWS, 128), F32),
            buf((DATA_ROWS, 128), F32),
            buf((2, MSG_ROWS, 128), F32),
            buf((MSG_ROWS, 128), F32),
            buf((16, 128), F32),
            buf((16, WIDTH), F32),
            buf((16, WIDTH), F32),
            buf((16, WIDTH), F32),
            dma((4,)),
            dma((4,)),
            dma((4,)),
            dma((4,)),
            dma((NCHUNK,)),
            dma((NCHUNK,)),
            dma((NCHUNK,)),
            dma((NCHUNK,)),
            dma((6,)),
            dma((6,)),
        ],
        compiler_params=pltpu.CompilerParams(
            collective_id=0, has_side_effects=True, vmem_limit_bytes=60 * 1024 * 1024
        ),
        name="moe",
    )(tokens, slot_keys, w_in, w_out, out_grad)
    keys_grad = keys_grad.reshape(KROWS, 2, 64).transpose(0, 2, 1).reshape(KROWS, 128)
    return layer_out, tokens_grad, keys_grad, w_in_grad, w_out_grad


def solution(mesh):
    placed = (
        P("tok", "grp"),
        P("tok", "grp"),
        P("grp", "tok", None, None),
        P("grp", "tok", None, None),
        P("tok", "grp"),
    )
    return jax.shard_map(
        body,
        mesh=mesh,
        in_specs=placed,
        out_specs=(
            P("tok", "grp"),
            P("tok", "grp"),
            P("tok", "grp"),
            P("grp", "tok", None, None),
            P("grp", "tok", None, None),
        ),
        check_vma=False,
    )
```

```python
import functools
import math

import jax
import jax.numpy as jnp
from jax import lax
from jax.experimental import pallas as pl
from jax.experimental.pallas import tpu as pltpu
from jax.sharding import PartitionSpec as P

MESH = pl.DeviceIdType.MESH
F32 = jnp.float32
BF16 = jnp.bfloat16

NT = 64
SIDE = 4
TOK = 2048
HALF = 768
WIDTH = 1536
HID = 1024
SLOTS = 256
SLOT_ROWS = 4
GROUPS6 = HALF // 128
DATA_ROWS = SLOT_ROWS * GROUPS6
CHUNK = 512
NCHUNK = TOK // CHUNK
KROWS = 24
PIECES = 4
LOWEST = -1e38

CONTRACT_ROWS = (((0,), (0,)), ((), ()))
CONTRACT_COLS = (((1,), (1,)), ((), ()))


def dot_nn(a, b):
    return jnp.dot(a, b, preferred_element_type=F32)


def dot_tn(a, b):
    return lax.dot_general(a, b, CONTRACT_ROWS, preferred_element_type=F32)


def dot_nt(a, b):
    return lax.dot_general(a, b, CONTRACT_COLS, preferred_element_type=F32)


def gelu_parts(v):
    cumulative = 0.5 * (1.0 + lax.erf(v * (1.0 / math.sqrt(2.0))))
    density = jnp.exp(-0.5 * v * v) * (1.0 / math.sqrt(2.0 * math.pi))
    return v * cumulative, cumulative + v * density


def rows_at(c):
    if isinstance(c, int):
        return pl.ds(c * CHUNK, CHUNK)
    return pl.ds(pl.multiple_of(c * CHUNK, CHUNK), CHUNK)


def each_chunk(step):
    lax.fori_loop(0, NCHUNK, lambda c, _: (step(c), 0)[1], 0)


def split_hi_lo(value, shape):
    lane = lax.broadcasted_iota(jnp.int32, shape, 1)
    hi = value.astype(BF16).astype(F32)
    return jnp.where(lane < 64, hi, value - hi)


def join_hi_lo(value):
    return value + pltpu.roll(value, 64, 1)


def kernel(
    tokens, keys, w_in, w_out, grads,
    lay_out, tok_out, key_out, win_out, wout_out,
    x, dy, wi, wo, wit, wot, part, logit, comb, combw, dispw, lgs, lgr, lg,
    acc, acc2, flat, keyf, keyown, keymsg, keyland, osgmsg, osgland, slotmsg, slotland, outmsg, outland,
    rtmsg, rtland, kgmsg, kgland, sval, rval, colmax, colsum,
    osgx, osgown, osgboth, slotx, outx, outr, rtx, arow, grow, srow,
    load_sem, out_sem, pair_s, pair_r, ls, lr, gs, gr, a2a_s, a2a_r,
):
    t = lax.axis_index("tok")
    g = lax.axis_index("grp")
    other = 1 - g
    cx, cy, cz = t // 16, lax.rem(t // 4, 4), lax.rem(t, 4)

    loads = [
        pltpu.make_async_copy(keys, keyown, load_sem.at[4]),
        pltpu.make_async_copy(tokens, x, load_sem.at[0]),
        pltpu.make_async_copy(grads, dy, load_sem.at[1]),
        pltpu.make_async_copy(w_out.at[0, 0], wo, load_sem.at[2]),
        pltpu.make_async_copy(w_in.at[0, 0], wi, load_sem.at[3]),
    ]
    for copy in loads:
        copy.start()

    barrier = pltpu.get_barrier_semaphore()

    def partner(i):
        a, b, c = i // 16, lax.rem(i // 4, 4), lax.rem(i, 4)
        px, py, pz = lax.rem(cx + 6 - a, 4), lax.rem(cy + 6 - b, 4), lax.rem(cz + 6 - c, 4)
        return px * 16 + py * 4 + pz

    def each_partner(send):
        def step(i, _):
            send(partner(i))
            return 0

        lax.fori_loop(0, 42, step, 0, unroll=True)
        lax.fori_loop(43, NT, step, 0, unroll=True)

    def greet(p):
        pl.semaphore_signal(barrier, inc=1, device_id={"tok": p, "grp": g}, device_id_type=MESH)
        pl.semaphore_signal(barrier, inc=1, device_id={"tok": p, "grp": other}, device_id_type=MESH)

    each_partner(greet)
    pl.semaphore_signal(barrier, inc=1, device_id={"tok": t, "grp": other}, device_id_type=MESH)

    row = lax.broadcasted_iota(jnp.int32, (128, 128), 0)
    col = lax.broadcasted_iota(jnp.int32, (128, 128), 1)
    loads[0].wait()
    order = jnp.where(row == 2 * lax.rem(col, 64) + col // 64, 1.0, 0.0).astype(BF16)
    keymsg[...] = dot_nn(keyown[...], order).astype(BF16)
    pl.semaphore_wait(barrier, 2 * NT - 1)

    def pair_copy(i, src, dst):
        return pltpu.make_async_remote_copy(
            src, dst, pair_s.at[i], pair_r.at[i], device_id={"tok": t, "grp": other}, device_id_type=MESH
        )

    def landed(i, buffer):
        pltpu.make_async_copy(buffer, buffer, a2a_r.at[i]).wait()

    def sent(i, block):
        pltpu.make_async_copy(block, block, a2a_s.at[i]).wait()

    half = t // 32
    place = g * 32 + lax.rem(t, 32)

    def send_keys(p):
        pltpu.make_async_remote_copy(
            keymsg, keyland.at[place], a2a_s.at[0], a2a_r.at[0],
            device_id={"tok": p, "grp": half}, device_id_type=MESH,
        ).start()

    each_partner(send_keys)

    @pl.when(half == g)
    def _():
        pltpu.make_async_copy(keymsg, keyland.at[place], a2a_r.at[0]).start()

    @pl.when(half != g)
    def _():
        pltpu.make_async_remote_copy(
            keymsg, keyland.at[place], a2a_s.at[0], a2a_r.at[0],
            device_id={"tok": t, "grp": other}, device_id_type=MESH,
        ).start()

    loads[3].wait()

    def turn_out(i, _):
        at = pl.ds(pl.multiple_of(i * 256, 256), 256)
        wot[:, at] = wo[at, :].T
        return 0

    lax.fori_loop(0, HID // 256, turn_out, 0)
    loads[4].wait()

    def turn_in(i, _):
        at = pl.ds(pl.multiple_of(i * 256, 256), 256)
        wit[:, at] = wi[at, :].T
        return 0

    lax.fori_loop(0, WIDTH // 256, turn_in, 0)

    landed(0, keyland)
    for h in range(2):
        block = keyland[h * 32:(h + 1) * 32, :, :].astype(F32)
        keyf[:, h * 128:(h + 1) * 128] = block.reshape(HALF, 128).astype(BF16)

    def logit_copy(c, group):
        lanes = pl.ds(128 * group, 128)
        return pltpu.make_async_remote_copy(
            part.at[rows_at(c), lanes], logit.at[rows_at(c), lanes],
            ls.at[group, c], lr.at[group, c],
            device_id={"tok": t, "grp": other}, device_id_type=MESH,
        )

    loads[1].wait()

    def logits_step(c):
        part[rows_at(c), :] = dot_nn(x[rows_at(c), :], keyf[...])
        logit_copy(c, 0).start()

    each_chunk(logits_step)
    each_chunk(lambda c: logit_copy(c, 1).start())

    for group in range(2):
        lanes = slice(128 * group, 128 * (group + 1))
        colmax[...] = jnp.full((8, 128), LOWEST, F32)
        colsum[...] = jnp.zeros((8, 128), F32)
        acc2[...] = jnp.zeros((128, HALF), F32)

        def disp_step(c):
            rows = rows_at(c)
            logit_copy(c, group).wait_recv()
            values = logit[rows, lanes] + part[rows, lanes]
            logit[rows, lanes] = values
            peak = jnp.max(jnp.max(values.reshape(CHUNK // 8, 8, 128), axis=0), axis=0, keepdims=True)
            peak = jnp.maximum(peak, colmax[0:1, :]).astype(BF16).astype(F32)
            weights = jnp.exp(values - peak)
            sums = jnp.sum(weights.reshape(CHUNK // 8, 8, 128), axis=0)
            rows_sum = dot_tn(weights.astype(BF16), x[rows, :])
            shift = jnp.exp(colmax[0:1, :] - peak)
            shift_col = jnp.broadcast_to(shift, (128, 128)).T
            for q in range(GROUPS6):
                at = slice(128 * q, 128 * (q + 1))
                acc2[:, at] = acc2[:, at] * shift_col + rows_sum[:, at]
            colsum[...] = colsum[...] * shift + sums
            colmax[0:1, :] = peak

        each_chunk(disp_step)

        peak_col = jnp.broadcast_to(colmax[0:1, :], (128, 128)).T
        total = jnp.sum(colsum[...], axis=0, keepdims=True)
        total_col = split_hi_lo(jnp.broadcast_to(total, (128, 128)).T, (128, 128))
        stat = jnp.where(g == 0, peak_col, total_col)
        for j in range(2):
            for q in range(GROUPS6):
                flat[pl.ds(2 * q + j, NT, stride=24), :] = acc2[64 * j:64 * (j + 1), 128 * q:128 * (q + 1)]
            flat[pl.ds(12 + j, NT, stride=24), :] = stat[64 * j:64 * (j + 1), :]
            flat[pl.ds(14 + j, NT, stride=24), :] = stat[64 * j:64 * (j + 1), :]
        slotmsg[group, :, :, :] = flat[0:NT * 24, :].reshape(NT, 24, 128)[:, 0:16, :].astype(BF16)

        def send_slots(p, group=group):
            pltpu.make_async_remote_copy(
                slotmsg.at[group, p], slotland.at[g, t], a2a_s.at[2], a2a_r.at[2],
                device_id={"tok": p, "grp": group}, device_id_type=MESH,
            ).start()

        each_partner(send_slots)

        @pl.when(g == group)
        def _():
            pltpu.make_async_copy(slotmsg.at[group, t], slotland.at[g, t], a2a_r.at[2]).start()

        @pl.when(g != group)
        def _():
            send_slots(t)

    def from_messages(dst, land):
        flat[0:NT * DATA_ROWS, :] = land[...].astype(F32).reshape(NT * DATA_ROWS, 128)
        for j in range(SLOT_ROWS):
            for q in range(GROUPS6):
                r = (j // 2) * 12 + 2 * q + j % 2
                dst[64 * j:64 * (j + 1), 128 * q:128 * (q + 1)] = (
                    flat[pl.ds(r, NT, stride=DATA_ROWS), :].astype(BF16)
                )

    def scatter(i, msg, land):
        def send(p):
            pltpu.make_async_remote_copy(
                msg.at[p], land.at[t], a2a_s.at[i], a2a_r.at[i],
                device_id={"tok": p, "grp": g}, device_id_type=MESH,
            ).start()

        each_partner(send)
        pltpu.make_async_copy(msg.at[t], land.at[t], a2a_r.at[i]).start()

    def spread(i, msg, land):
        def send(p):
            pltpu.make_async_remote_copy(
                msg, land.at[t], a2a_s.at[i], a2a_r.at[i],
                device_id={"tok": p, "grp": g}, device_id_type=MESH,
            ).start()

        each_partner(send)
        pltpu.make_async_copy(msg, land.at[t], a2a_r.at[i]).start()

    loads[2].wait()
    def comb_step(c):
        rows = rows_at(c)
        values = logit[rows, :]
        weights = jnp.exp(values - jnp.max(values, axis=1, keepdims=True))
        weights = weights / jnp.sum(weights, axis=1, keepdims=True)
        comb[rows, :] = weights
        combw[rows, :] = weights.astype(BF16)

    each_chunk(comb_step)
    acc[...] = jnp.zeros((SLOTS, HALF), F32)

    def slot_grad_step(c):
        acc[...] += dot_tn(combw[rows_at(c), :], dy[rows_at(c), :])

    each_chunk(slot_grad_step)
    osgown[...] = acc[...].astype(BF16)
    osg_pair = pair_copy(0, osgown.at[pl.ds(pl.multiple_of(other * 128, 128), 128)], osgboth.at[g])
    osg_pair.start()
    osgboth[g, :, :] = osgown[pl.ds(pl.multiple_of(g * 128, 128), 128), :]
    osg_pair.wait_recv()
    for h in range(2):
        for j in range(2):
            for q in range(GROUPS6):
                value = osgboth[h, 64 * j:64 * (j + 1), 128 * q:128 * (q + 1)]
                flat[pl.ds((h * GROUPS6 + q) * 2 + j, NT, stride=DATA_ROWS), :] = value.astype(F32)
    osgmsg[...] = flat[0:NT * DATA_ROWS, :].reshape(NT, DATA_ROWS, 128).astype(BF16)
    scatter(1, osgmsg, osgland)

    row16 = lax.broadcasted_iota(jnp.int32, (16, 1), 0)

    def to_rows(dst, block_of):
        dst[...] = jnp.zeros((16, WIDTH), F32)
        for at in range(WIDTH // 128):
            dst[0:2, 128 * at:128 * (at + 1)] = block_of(at)

    landed(2, slotland)
    tail0 = slotland[0, :, 8:16, :].astype(F32)
    tail1 = slotland[1, :, 8:16, :].astype(F32)
    row8 = lax.broadcasted_iota(jnp.int32, (NT, 8, 128), 1)
    swapped = jnp.concatenate([tail0[:, 4:8, :], tail0[:, 0:4, :]], axis=1)
    peaks = jnp.where(row8 < 4, swapped, tail0)
    top = jnp.max(peaks, axis=0)
    scale = jnp.exp(peaks - top[None])
    whole = join_hi_lo(jnp.sum(scale * tail1, axis=0))
    whole = jnp.concatenate([whole[4:8, :], whole[4:8, :]], axis=0)
    for h, tail in ((0, tail0), (1, tail1)):
        head = slotland[h, :, 0:8, :].astype(F32)
        slotx[h, 0:8, :] = jnp.sum(head * scale, axis=0) / whole
        slotx[h, 8:16, :] = jnp.sum(tail * scale, axis=0) / whole
    to_rows(srow, lambda at: slotx[at // GROUPS6, 2 * (at % GROUPS6):2 * (at % GROUPS6) + 2, :])
    slot_in = srow[...].astype(BF16)
    pre_act = dot_nn(slot_in, wi[...])
    hidden, slope = gelu_parts(pre_act)
    hidden = hidden.astype(BF16)
    slot_out = dot_nn(hidden, wo[...])
    for at in range(WIDTH // 128):
        h, q = at // GROUPS6, at % GROUPS6
        outx[h, 2 * q:2 * q + 2, :] = slot_out[0:2, 128 * at:128 * (at + 1)]
    out_pair = pair_copy(2, outx.at[other], outr.at[g])
    out_pair.start()
    outr[g, :, :] = outx[g, :, :]
    out_pair.wait_recv()
    outmsg[...] = jnp.concatenate([outr[0, 0:12, :], outr[1, 0:12, :]], axis=0).astype(BF16)
    spread(3, outmsg, outland)

    landed(1, osgland)
    osgx[...] = jnp.sum(osgland[...].astype(F32), axis=0)
    to_rows(grow, lambda at: osgx[2 * at:2 * at + 2, :])
    out_grad = grow[...].astype(BF16)
    hidden_grad = dot_nn(out_grad, wot[...])
    pre_grad = (hidden_grad * slope).astype(BF16)
    slot_in_grad = dot_nn(pre_grad, wit[...])
    arow[...] = jnp.zeros((16, 128), F32)
    arow[0:2, :] = whole[0:2, :]
    top_own = top[0:2, :]
    whole_rows = jnp.where(row16 < 2, arow[...], 1.0)
    routed = slot_in_grad / jnp.concatenate([whole_rows] * (WIDTH // 128), axis=1)
    routed = routed.astype(BF16).astype(F32)
    products = srow[...] * routed
    lane4 = lax.broadcasted_iota(jnp.int32, (2, 128), 1)
    for h in range(2):
        share = jnp.sum(products[:, h * HALF:(h + 1) * HALF], axis=1, keepdims=True)
        own = [routed[0:2, :], top_own, share[0:2, :]]
        for q in range(GROUPS6):
            at = (h * GROUPS6 + q) * 128
            rtx[h, 2 * q:2 * q + 2, :] = own[0][:, at:at + 128]
        rtx[h, 12:14, :] = own[1]
        value = jnp.broadcast_to(own[2], (2, 128))
        high = value.astype(BF16).astype(F32)
        rtx[h, 14:16, :] = jnp.where(lane4 < 64, high, value - high)
    rtmsg[...] = rtx[...].astype(BF16)

    def send_routed(p):
        for h, core in ((0, 0), (1, 1)):
            pltpu.make_async_remote_copy(
                rtmsg.at[h], rtland.at[g, t], a2a_s.at[4], a2a_r.at[4],
                device_id={"tok": p, "grp": core}, device_id_type=MESH,
            ).start()

    each_partner(send_routed)
    pltpu.make_async_remote_copy(
        rtmsg.at[other], rtland.at[g, t], a2a_s.at[4], a2a_r.at[4],
        device_id={"tok": t, "grp": other}, device_id_type=MESH,
    ).start()
    pltpu.make_async_copy(rtmsg.at[g], rtland.at[g, t], a2a_r.at[4]).start()

    wout_out[0, 0] = dot_tn(hidden, out_grad).astype(BF16)
    win_out[0, 0] = dot_tn(slot_in, pre_grad).astype(BF16)

    landed(3, outland)
    from_messages(sval, outland)

    def out_step(c):
        rows = rows_at(c)
        lay_out[rows, :] = dot_nn(combw[rows, :], sval[...]).astype(BF16)
        weights = comb[rows, :]
        out_dot = dot_nt(dy[rows, :], sval[...])
        mix = jnp.sum(weights * out_dot, axis=1, keepdims=True)
        comb[rows, :] = weights * (out_dot - mix)

    each_chunk(out_step)

    landed(4, rtland)
    flat[0:2 * NT * 16, :] = rtland[...].astype(F32).reshape(2 * NT * 16, 128)

    def routed_rows(j, r):
        return flat[pl.ds((j // 2) * NT * 16 + r + j % 2, NT, stride=16), :]

    for j in range(SLOT_ROWS):
        for q in range(GROUPS6):
            rval[64 * j:64 * (j + 1), 128 * q:128 * (q + 1)] = routed_rows(j, 2 * q).astype(BF16)
    top_row = jnp.concatenate([routed_rows(j, 12) for j in range(SLOT_ROWS)], axis=0).T[0:1, :]
    lane_sum = jnp.concatenate([routed_rows(j, 14) for j in range(SLOT_ROWS)], axis=0)
    disp_dot = join_hi_lo(lane_sum).T[0:1, :]

    def grad_copy(c):
        return pltpu.make_async_remote_copy(
            lgs.at[rows_at(c)], lgr.at[rows_at(c)], gs.at[c], gr.at[c],
            device_id={"tok": t, "grp": other}, device_id_type=MESH,
        )

    def in_step(c):
        rows = rows_at(c)
        weights = jnp.exp(logit[rows, :] - top_row)
        dispw[rows, :] = weights.astype(BF16)
        in_dot = dot_nt(x[rows, :], rval[...])
        lgs[rows, :] = (comb[rows, :] + weights * (in_dot - disp_dot)).astype(BF16)
        grad_copy(c).start()

    each_chunk(in_step)
    acc[...] = jnp.zeros((SLOTS, HALF), F32)

    def keys_step(c):
        rows = rows_at(c)
        grad_copy(c).wait_recv()
        low = (lgs[rows, :].astype(F32) + lgr[rows, :].astype(F32)).astype(BF16)
        lg[rows, :] = low
        acc[...] += dot_tn(low, x[rows, :])

    each_chunk(keys_step)

    for h in range(2):
        for q in range(GROUPS6):
            turned = acc[h * 128:(h + 1) * 128, q * 128:(q + 1) * 128].T
            flat[h * HALF + q * 128:h * HALF + (q + 1) * 128, :] = turned
    kgmsg[...] = flat[0:2 * HALF, :].reshape(NT, KROWS, 128).astype(BF16)

    def key_target(i):
        b, c, a, d = i // 16, lax.rem(i // 4, 4), lax.rem(i // 2, 2), lax.rem(i, 2)
        px, py, pz = lax.rem(cx + a, 2), lax.rem(cy + 6 - b, 4), lax.rem(cz + 6 - c, 4)
        return px * 16 + py * 4 + pz, lax.rem(g + d, 2)

    def grad_send(i):
        p, d = key_target(i)
        return pltpu.make_async_remote_copy(
            kgmsg.at[d * 32 + p], kgland.at[t], a2a_s.at[5], a2a_r.at[5],
            device_id={"tok": g * 32 + p, "grp": d}, device_id_type=MESH,
        )

    def send_grad(i, _):
        grad_send(i).start()
        return 0

    def send_near(i, _):
        p, d = key_target(i)

        @pl.when((g * 32 + p != t) | (d != g))
        def _():
            grad_send(i).start()

        return 0

    lax.fori_loop(0, 40, send_grad, 0, unroll=True)
    lax.fori_loop(44, NT, send_grad, 0, unroll=True)
    lax.fori_loop(40, 44, send_near, 0)

    @pl.when(half == g)
    def _():
        pltpu.make_async_copy(kgmsg.at[g * 32 + lax.rem(t, 32)], kgland.at[t], a2a_r.at[5]).start()

    def tok_step(c):
        rows = rows_at(c)
        value = dot_nn(dispw[rows, :], rval[...]) + dot_nt(lg[rows, :], keyf[...])
        tok_out[rows, :] = value.astype(BF16)

    each_chunk(tok_step)

    landed(5, kgland)
    turned = jnp.sum(kgland[...].astype(F32), axis=0)
    parts = []
    for _ in range(3):
        parts.append(turned.astype(BF16))
        turned = turned - parts[-1].astype(F32)
    key_out[...] = dot_nt(parts[0], order) + (dot_nt(parts[1], order) + dot_nt(parts[2], order))

    for pair in (osg_pair, out_pair):
        pair.wait_send()

    for c in range(NCHUNK):
        logit_copy(c, 0).wait_send()
        logit_copy(c, 1).wait_send()
        grad_copy(c).wait_send()
    sent(1, osgmsg.at[pl.ds(0, NT - 1)])
    sent(2, slotland.at[0])
    sent(2, slotland.at[1, pl.ds(0, NT - 1)])
    sent(3, outland.at[pl.ds(0, NT - 1)])
    sent(4, rtland.at[0])
    sent(4, rtland.at[1, pl.ds(0, NT - 1)])

    @pl.when(half == g)
    def _():
        sent(0, keyland.at[pl.ds(0, NT - 1)])
        sent(5, kgmsg.at[pl.ds(0, NT - 1)])

    @pl.when(half != g)
    def _():
        sent(0, keyland)
        sent(5, kgmsg)


def store(lay, tok, key, win, wout, lay_out, tok_out, key_out, win_out, wout_out, sems):
    pairs = [(key, key_out)]
    for i in range(PIECES):
        rows = pl.ds(i * (TOK // PIECES), TOK // PIECES)
        pairs += [(lay.at[rows], lay_out.at[rows]), (tok.at[rows], tok_out.at[rows])]
        rows = pl.ds(i * (WIDTH // PIECES), WIDTH // PIECES)
        pairs.append((win.at[0, 0, rows], win_out.at[0, 0, rows]))
        rows = pl.ds(i * (HID // PIECES), HID // PIECES)
        pairs.append((wout.at[0, 0, rows], wout_out.at[0, 0, rows]))
    copies = [pltpu.make_async_copy(src, dst, sems.at[i]) for i, (src, dst) in enumerate(pairs)]
    for copy in copies:
        copy.start()
    for copy in copies:
        copy.wait()


def body(tokens, slot_keys, w_in, w_out, out_grad):
    anywhere = pl.BlockSpec(memory_space=pl.ANY)
    vmem = pl.BlockSpec(memory_space=pltpu.VMEM)
    buf = pltpu.VMEM
    dma = pltpu.SemaphoreType.DMA
    paired = buf((2, NT, 16, 128), BF16)
    short = buf((NT, DATA_ROWS, 128), BF16)
    layer_out, tokens_grad, keys_grad, w_in_grad, w_out_grad = pl.pallas_call(
        kernel,
        out_shape=(
            pltpu.VMEM((TOK, HALF), BF16),
            pltpu.VMEM((TOK, HALF), BF16),
            pltpu.VMEM((KROWS, 128), F32),
            pltpu.VMEM(w_in.shape, BF16),
            pltpu.VMEM(w_out.shape, BF16),
        ),
        in_specs=[anywhere] * 5,
        out_specs=[vmem, vmem, vmem, vmem, vmem],
        scratch_shapes=[
            buf((TOK, HALF), BF16),
            buf((TOK, HALF), BF16),
            buf((WIDTH, HID), BF16),
            buf((HID, WIDTH), BF16),
            buf((HID, WIDTH), BF16),
            buf((WIDTH, HID), BF16),
            buf((TOK, SLOTS), F32),
            buf((TOK, SLOTS), F32),
            buf((TOK, SLOTS), F32),
            buf((TOK, SLOTS), BF16),
            buf((TOK, SLOTS), BF16),
            buf((TOK, SLOTS), BF16),
            buf((TOK, SLOTS), BF16),
            buf((TOK, SLOTS), BF16),
            buf((SLOTS, HALF), F32),
            buf((128, HALF), F32),
            buf((2 * NT * 16, 128), F32),
            buf((HALF, SLOTS), BF16),
            buf((KROWS, 128), BF16),
            buf((KROWS, 128), BF16),
            short,
            short,
            short,
            paired,
            paired,
            buf((DATA_ROWS, 128), BF16),
            short,
            buf((2, 16, 128), BF16),
            paired,
            short,
            short,
            buf((SLOTS, HALF), BF16),
            buf((SLOTS, HALF), BF16),
            buf((8, 128), F32),
            buf((8, 128), F32),
            buf((DATA_ROWS, 128), F32),
            buf((SLOTS, HALF), BF16),
            buf((2, 128, HALF), BF16),
            buf((2, 16, 128), F32),
            buf((2, 16, 128), F32),
            buf((2, 16, 128), F32),
            buf((2, 16, 128), F32),
            buf((16, 128), F32),
            buf((16, WIDTH), F32),
            buf((16, WIDTH), F32),
            dma((5,)),
            dma((4,)),
            dma((4,)),
            dma((4,)),
            dma((2, NCHUNK)),
            dma((2, NCHUNK)),
            dma((NCHUNK,)),
            dma((NCHUNK,)),
            dma((6,)),
            dma((6,)),
        ],
        compiler_params=pltpu.CompilerParams(
            collective_id=0, has_side_effects=True, vmem_limit_bytes=46 * 1024 * 1024
        ),
        name="moe",
    )(tokens, slot_keys, w_in, w_out, out_grad)
    results = (layer_out, tokens_grad, keys_grad, w_in_grad, w_out_grad)
    results = tuple(pltpu.with_memory_space_constraint(r, pltpu.VMEM) for r in results)
    return pl.pallas_call(
        store,
        out_shape=tuple(jax.ShapeDtypeStruct(r.shape, r.dtype) for r in results),
        in_specs=[vmem] * 5,
        out_specs=[anywhere] * 5,
        scratch_shapes=[dma((4 * PIECES + 1,))],
        compiler_params=pltpu.CompilerParams(has_side_effects=True, vmem_limit_bytes=1024 * 1024),
        name="store",
    )(*results)


def solution(mesh):
    placed = (
        P("tok", "grp"),
        P("tok", "grp"),
        P("grp", "tok", None, None),
        P("grp", "tok", None, None),
        P("tok", "grp"),
    )
    return jax.shard_map(
        body,
        mesh=mesh,
        in_specs=placed,
        out_specs=(
            P("tok", "grp"),
            P("tok", "grp"),
            P("tok", "grp"),
            P("grp", "tok", None, None),
            P("grp", "tok", None, None),
        ),
        check_vma=False,
    )
```

```python
import functools
import math

import jax
import jax.numpy as jnp
from jax import lax
from jax.experimental import pallas as pl
from jax.experimental.pallas import tpu as pltpu
from jax.sharding import PartitionSpec as P

MESH = pl.DeviceIdType.MESH
F32 = jnp.float32
BF16 = jnp.bfloat16

NT = 64
SIDE = 4
TOK = 2048
HALF = 768
WIDTH = 1536
HID = 1024
SLOTS = 256
SLOT_ROWS = 4
GROUPS6 = HALF // 128
DATA_ROWS = SLOT_ROWS * GROUPS6
CHUNK = 512
NCHUNK = TOK // CHUNK
KROWS = 24
PIECES = 4
LOWEST = -1e38

CONTRACT_ROWS = (((0,), (0,)), ((), ()))
CONTRACT_COLS = (((1,), (1,)), ((), ()))


def dot_nn(a, b):
    return jnp.dot(a, b, preferred_element_type=F32)


def dot_tn(a, b):
    return lax.dot_general(a, b, CONTRACT_ROWS, preferred_element_type=F32)


def dot_nt(a, b):
    return lax.dot_general(a, b, CONTRACT_COLS, preferred_element_type=F32)


def gelu_parts(v):
    cumulative = 0.5 * (1.0 + lax.erf(v * (1.0 / math.sqrt(2.0))))
    density = jnp.exp(-0.5 * v * v) * (1.0 / math.sqrt(2.0 * math.pi))
    return v * cumulative, cumulative + v * density


def rows_at(c):
    if isinstance(c, int):
        return pl.ds(c * CHUNK, CHUNK)
    return pl.ds(pl.multiple_of(c * CHUNK, CHUNK), CHUNK)


def each_chunk(step):
    lax.fori_loop(0, NCHUNK, lambda c, _: (step(c), 0)[1], 0)


def split_hi_lo(value, shape):
    lane = lax.broadcasted_iota(jnp.int32, shape, 1)
    hi = value.astype(BF16).astype(F32)
    return jnp.where(lane < 64, hi, value - hi)


def join_hi_lo(value):
    return value + pltpu.roll(value, 64, 1)


def kernel(
    tokens, keys, w_in, w_out, grads,
    lay_out, tok_out, key_out, win_out, wout_out,
    x, dy, wi, wo, wit, wot, part, logit, comb, combw, dispw, lgs, lgr, lg,
    acc, acc2, flat, keyf, keyown, keymsg, keyland, osgmsg, osgland, slotmsg, slotland, outmsg, outland,
    rtmsg, rtland, kgmsg, kgland, sval, rval, colmax, colsum,
    osgx, osgown, osgboth, slotx, outx, outr, rtx, arow, grow, srow,
    load_sem, out_sem, pair_s, pair_r, ls, lr, gs, gr, a2a_s, a2a_r,
):
    t = lax.axis_index("tok")
    g = lax.axis_index("grp")
    other = 1 - g
    cx, cy, cz = t // 16, lax.rem(t // 4, 4), lax.rem(t, 4)

    loads = [
        pltpu.make_async_copy(keys, keyown, load_sem.at[4]),
        pltpu.make_async_copy(tokens, x, load_sem.at[0]),
        pltpu.make_async_copy(grads, dy, load_sem.at[1]),
        pltpu.make_async_copy(w_out.at[0, 0], wo, load_sem.at[2]),
        pltpu.make_async_copy(w_in.at[0, 0], wi, load_sem.at[3]),
    ]
    for copy in loads:
        copy.start()

    barrier = pltpu.get_barrier_semaphore()

    def partner(i):
        a, b, c = i // 16, lax.rem(i // 4, 4), lax.rem(i, 4)
        px, py, pz = lax.rem(cx + 6 - a, 4), lax.rem(cy + 6 - b, 4), lax.rem(cz + 6 - c, 4)
        return px * 16 + py * 4 + pz

    def each_partner(send):
        def step(i, _):
            send(partner(i))
            return 0

        lax.fori_loop(0, 42, step, 0, unroll=True)
        lax.fori_loop(43, NT, step, 0, unroll=True)

    def greet(p):
        pl.semaphore_signal(barrier, inc=1, device_id={"tok": p, "grp": g}, device_id_type=MESH)
        pl.semaphore_signal(barrier, inc=1, device_id={"tok": p, "grp": other}, device_id_type=MESH)

    each_partner(greet)
    pl.semaphore_signal(barrier, inc=1, device_id={"tok": t, "grp": other}, device_id_type=MESH)

    row = lax.broadcasted_iota(jnp.int32, (128, 128), 0)
    col = lax.broadcasted_iota(jnp.int32, (128, 128), 1)
    loads[0].wait()
    order = jnp.where(row == 2 * lax.rem(col, 64) + col // 64, 1.0, 0.0).astype(BF16)
    keymsg[...] = dot_nn(keyown[...], order).astype(BF16)
    pl.semaphore_wait(barrier, 2 * NT - 1)

    def pair_copy(i, src, dst):
        return pltpu.make_async_remote_copy(
            src, dst, pair_s.at[i], pair_r.at[i], device_id={"tok": t, "grp": other}, device_id_type=MESH
        )

    def landed(i, buffer):
        pltpu.make_async_copy(buffer, buffer, a2a_r.at[i]).wait()

    def sent(i, block):
        pltpu.make_async_copy(block, block, a2a_s.at[i]).wait()

    half = t // 32
    place = g * 32 + lax.rem(t, 32)

    def send_keys(p):
        pltpu.make_async_remote_copy(
            keymsg, keyland.at[place], a2a_s.at[0], a2a_r.at[0],
            device_id={"tok": p, "grp": half}, device_id_type=MESH,
        ).start()

    each_partner(send_keys)

    @pl.when(half == g)
    def _():
        pltpu.make_async_copy(keymsg, keyland.at[place], a2a_r.at[0]).start()

    @pl.when(half != g)
    def _():
        pltpu.make_async_remote_copy(
            keymsg, keyland.at[place], a2a_s.at[0], a2a_r.at[0],
            device_id={"tok": t, "grp": other}, device_id_type=MESH,
        ).start()

    loads[3].wait()

    def turn_out(i, _):
        at = pl.ds(pl.multiple_of(i * 256, 256), 256)
        wot[:, at] = wo[at, :].T
        return 0

    lax.fori_loop(0, HID // 256, turn_out, 0)
    loads[4].wait()

    def turn_in(i, _):
        at = pl.ds(pl.multiple_of(i * 256, 256), 256)
        wit[:, at] = wi[at, :].T
        return 0

    lax.fori_loop(0, WIDTH // 256, turn_in, 0)

    landed(0, keyland)
    for h in range(2):
        block = keyland[h * 32:(h + 1) * 32, :, :].astype(F32)
        keyf[:, h * 128:(h + 1) * 128] = block.reshape(HALF, 128).astype(BF16)

    def logit_copy(c, group):
        lanes = pl.ds(128 * group, 128)
        return pltpu.make_async_remote_copy(
            part.at[rows_at(c), lanes], logit.at[rows_at(c), lanes],
            ls.at[group, c], lr.at[group, c],
            device_id={"tok": t, "grp": other}, device_id_type=MESH,
        )

    loads[1].wait()

    def logits_step(c):
        part[rows_at(c), :] = dot_nn(x[rows_at(c), :], keyf[...])
        logit_copy(c, 0).start()

    each_chunk(logits_step)
    each_chunk(lambda c: logit_copy(c, 1).start())

    for group in range(2):
        lanes = slice(128 * group, 128 * (group + 1))
        colmax[...] = jnp.full((8, 128), LOWEST, F32)
        colsum[...] = jnp.zeros((8, 128), F32)
        acc2[...] = jnp.zeros((128, HALF), F32)

        def disp_step(c):
            rows = rows_at(c)
            logit_copy(c, group).wait_recv()
            values = logit[rows, lanes] + part[rows, lanes]
            logit[rows, lanes] = values
            peak = jnp.max(jnp.max(values.reshape(CHUNK // 8, 8, 128), axis=0), axis=0, keepdims=True)
            peak = jnp.maximum(peak, colmax[0:1, :]).astype(BF16).astype(F32)
            weights = jnp.exp(values - peak)
            sums = jnp.sum(weights.reshape(CHUNK // 8, 8, 128), axis=0)
            rows_sum = dot_tn(weights.astype(BF16), x[rows, :])
            shift = jnp.exp(colmax[0:1, :] - peak)
            shift_col = jnp.broadcast_to(shift, (128, 128)).T
            for q in range(GROUPS6):
                at = slice(128 * q, 128 * (q + 1))
                acc2[:, at] = acc2[:, at] * shift_col + rows_sum[:, at]
            colsum[...] = colsum[...] * shift + sums
            colmax[0:1, :] = peak

        each_chunk(disp_step)

        peak_col = jnp.broadcast_to(colmax[0:1, :], (128, 128)).T
        total = jnp.sum(colsum[...], axis=0, keepdims=True)
        total_col = split_hi_lo(jnp.broadcast_to(total, (128, 128)).T, (128, 128))
        stat = jnp.where(g == 0, peak_col, total_col)
        for j in range(2):
            for q in range(GROUPS6):
                flat[pl.ds(2 * q + j, NT, stride=24), :] = acc2[64 * j:64 * (j + 1), 128 * q:128 * (q + 1)]
            flat[pl.ds(12 + j, NT, stride=24), :] = stat[64 * j:64 * (j + 1), :]
            flat[pl.ds(14 + j, NT, stride=24), :] = stat[64 * j:64 * (j + 1), :]
        slotmsg[group, :, :, :] = flat[0:NT * 24, :].reshape(NT, 24, 128)[:, 0:16, :].astype(BF16)

        def send_slots(p, group=group):
            pltpu.make_async_remote_copy(
                slotmsg.at[group, p], slotland.at[g, t], a2a_s.at[2], a2a_r.at[2],
                device_id={"tok": p, "grp": group}, device_id_type=MESH,
            ).start()

        each_partner(send_slots)

        @pl.when(g == group)
        def _():
            pltpu.make_async_copy(slotmsg.at[group, t], slotland.at[g, t], a2a_r.at[2]).start()

        @pl.when(g != group)
        def _():
            send_slots(t)

    def from_messages(dst, land):
        flat[0:NT * DATA_ROWS, :] = land[...].astype(F32).reshape(NT * DATA_ROWS, 128)
        for j in range(SLOT_ROWS):
            for q in range(GROUPS6):
                r = (j // 2) * 12 + 2 * q + j % 2
                dst[64 * j:64 * (j + 1), 128 * q:128 * (q + 1)] = (
                    flat[pl.ds(r, NT, stride=DATA_ROWS), :].astype(BF16)
                )

    def scatter(i, msg, land):
        def send(p):
            pltpu.make_async_remote_copy(
                msg.at[p], land.at[t], a2a_s.at[i], a2a_r.at[i],
                device_id={"tok": p, "grp": g}, device_id_type=MESH,
            ).start()

        each_partner(send)
        pltpu.make_async_copy(msg.at[t], land.at[t], a2a_r.at[i]).start()

    def spread(i, msg, land):
        def send(p):
            pltpu.make_async_remote_copy(
                msg, land.at[t], a2a_s.at[i], a2a_r.at[i],
                device_id={"tok": p, "grp": g}, device_id_type=MESH,
            ).start()

        each_partner(send)
        pltpu.make_async_copy(msg, land.at[t], a2a_r.at[i]).start()

    loads[2].wait()
    def comb_step(c):
        rows = rows_at(c)
        values = logit[rows, :]
        weights = jnp.exp(values - jnp.max(values, axis=1, keepdims=True))
        weights = weights / jnp.sum(weights, axis=1, keepdims=True)
        comb[rows, :] = weights
        combw[rows, :] = weights.astype(BF16)

    each_chunk(comb_step)
    acc[...] = jnp.zeros((SLOTS, HALF), F32)

    def slot_grad_step(c):
        acc[...] += dot_tn(combw[rows_at(c), :], dy[rows_at(c), :])

    each_chunk(slot_grad_step)
    osgown[...] = acc[...].astype(BF16)
    osg_pair = pair_copy(0, osgown.at[pl.ds(pl.multiple_of(other * 128, 128), 128)], osgboth.at[g])
    osg_pair.start()
    osgboth[g, :, :] = osgown[pl.ds(pl.multiple_of(g * 128, 128), 128), :]
    osg_pair.wait_recv()
    for h in range(2):
        for j in range(2):
            for q in range(GROUPS6):
                value = osgboth[h, 64 * j:64 * (j + 1), 128 * q:128 * (q + 1)]
                flat[pl.ds((h * GROUPS6 + q) * 2 + j, NT, stride=DATA_ROWS), :] = value.astype(F32)
    osgmsg[...] = flat[0:NT * DATA_ROWS, :].reshape(NT, DATA_ROWS, 128).astype(BF16)
    scatter(1, osgmsg, osgland)

    row16 = lax.broadcasted_iota(jnp.int32, (16, 1), 0)

    def to_rows(dst, block_of):
        dst[...] = jnp.zeros((16, WIDTH), F32)
        for at in range(WIDTH // 128):
            dst[0:2, 128 * at:128 * (at + 1)] = block_of(at)

    landed(2, slotland)
    tail0 = slotland[0, :, 8:16, :].astype(F32)
    tail1 = slotland[1, :, 8:16, :].astype(F32)
    row8 = lax.broadcasted_iota(jnp.int32, (NT, 8, 128), 1)
    swapped = jnp.concatenate([tail0[:, 4:8, :], tail0[:, 0:4, :]], axis=1)
    peaks = jnp.where(row8 < 4, swapped, tail0)
    top = jnp.max(peaks, axis=0)
    scale = jnp.exp(peaks - top[None])
    whole = join_hi_lo(jnp.sum(scale * tail1, axis=0))
    whole = jnp.concatenate([whole[4:8, :], whole[4:8, :]], axis=0)
    for h, tail in ((0, tail0), (1, tail1)):
        head = slotland[h, :, 0:8, :].astype(F32)
        slotx[h, 0:8, :] = jnp.sum(head * scale, axis=0) / whole
        slotx[h, 8:16, :] = jnp.sum(tail * scale, axis=0) / whole
    to_rows(srow, lambda at: slotx[at // GROUPS6, 2 * (at % GROUPS6):2 * (at % GROUPS6) + 2, :])
    slot_in = srow[...].astype(BF16)
    pre_act = dot_nn(slot_in, wi[...])
    hidden, slope = gelu_parts(pre_act)
    hidden = hidden.astype(BF16)
    slot_out = dot_nn(hidden, wo[...])
    for at in range(WIDTH // 128):
        h, q = at // GROUPS6, at % GROUPS6
        outx[h, 2 * q:2 * q + 2, :] = slot_out[0:2, 128 * at:128 * (at + 1)]
    out_pair = pair_copy(2, outx.at[other], outr.at[g])
    out_pair.start()
    outr[g, :, :] = outx[g, :, :]
    out_pair.wait_recv()
    outmsg[...] = jnp.concatenate([outr[0, 0:12, :], outr[1, 0:12, :]], axis=0).astype(BF16)
    spread(3, outmsg, outland)

    landed(1, osgland)
    osgx[...] = jnp.sum(osgland[...].astype(F32), axis=0)
    to_rows(grow, lambda at: osgx[2 * at:2 * at + 2, :])
    out_grad = grow[...].astype(BF16)
    hidden_grad = dot_nn(out_grad, wot[...])
    pre_grad = (hidden_grad * slope).astype(BF16)
    slot_in_grad = dot_nn(pre_grad, wit[...])
    arow[...] = jnp.zeros((16, 128), F32)
    arow[0:2, :] = whole[0:2, :]
    top_own = top[0:2, :]
    whole_rows = jnp.where(row16 < 2, arow[...], 1.0)
    routed = slot_in_grad / jnp.concatenate([whole_rows] * (WIDTH // 128), axis=1)
    routed = routed.astype(BF16).astype(F32)
    products = srow[...] * routed
    lane4 = lax.broadcasted_iota(jnp.int32, (2, 128), 1)
    for h in range(2):
        share = jnp.sum(products[:, h * HALF:(h + 1) * HALF], axis=1, keepdims=True)
        own = [routed[0:2, :], top_own, share[0:2, :]]
        for q in range(GROUPS6):
            at = (h * GROUPS6 + q) * 128
            rtx[h, 2 * q:2 * q + 2, :] = own[0][:, at:at + 128]
        rtx[h, 12:14, :] = own[1]
        value = jnp.broadcast_to(own[2], (2, 128))
        high = value.astype(BF16).astype(F32)
        rtx[h, 14:16, :] = jnp.where(lane4 < 64, high, value - high)
    rtmsg[...] = rtx[...].astype(BF16)

    def send_routed(p):
        for h, core in ((0, 0), (1, 1)):
            pltpu.make_async_remote_copy(
                rtmsg.at[h], rtland.at[g, t], a2a_s.at[4], a2a_r.at[4],
                device_id={"tok": p, "grp": core}, device_id_type=MESH,
            ).start()

    each_partner(send_routed)
    pltpu.make_async_remote_copy(
        rtmsg.at[other], rtland.at[g, t], a2a_s.at[4], a2a_r.at[4],
        device_id={"tok": t, "grp": other}, device_id_type=MESH,
    ).start()
    pltpu.make_async_copy(rtmsg.at[g], rtland.at[g, t], a2a_r.at[4]).start()

    wout_out[0, 0] = dot_tn(hidden, out_grad).astype(BF16)
    win_out[0, 0] = dot_tn(slot_in, pre_grad).astype(BF16)

    landed(3, outland)
    from_messages(sval, outland)

    def out_step(c):
        rows = rows_at(c)
        lay_out[rows, :] = dot_nn(combw[rows, :], sval[...]).astype(BF16)
        weights = comb[rows, :]
        out_dot = dot_nt(dy[rows, :], sval[...])
        mix = jnp.sum(weights * out_dot, axis=1, keepdims=True)
        comb[rows, :] = weights * (out_dot - mix)

    each_chunk(out_step)

    landed(4, rtland)
    flat[0:2 * NT * 16, :] = rtland[...].astype(F32).reshape(2 * NT * 16, 128)

    def routed_rows(j, r):
        return flat[pl.ds((j // 2) * NT * 16 + r + j % 2, NT, stride=16), :]

    for j in range(SLOT_ROWS):
        for q in range(GROUPS6):
            rval[64 * j:64 * (j + 1), 128 * q:128 * (q + 1)] = routed_rows(j, 2 * q).astype(BF16)
    top_row = jnp.concatenate([routed_rows(j, 12) for j in range(SLOT_ROWS)], axis=0).T[0:1, :]
    lane_sum = jnp.concatenate([routed_rows(j, 14) for j in range(SLOT_ROWS)], axis=0)
    disp_dot = join_hi_lo(lane_sum).T[0:1, :]

    def grad_copy(c, group):
        return pltpu.make_async_remote_copy(
            lgs.at[rows_at(c)], lgr.at[rows_at(c)], gs.at[group, c], gr.at[group, c],
            device_id={"tok": t, "grp": other}, device_id_type=MESH,
        )

    def in_step(c):
        rows = rows_at(c)
        weights = jnp.exp(logit[rows, :] - top_row)
        dispw[rows, :] = weights.astype(BF16)
        in_dot = dot_nt(x[rows, :], rval[...])
        lgs[rows, :] = (comb[rows, :] + weights * (in_dot - disp_dot)).astype(BF16)
        grad_copy(c, 0).start()

    each_chunk(in_step)

    def key_target(i):
        b, c, a = i // 8, lax.rem(i // 2, 4), lax.rem(i, 2)
        px, py, pz = lax.rem(cx + a, 2), lax.rem(cy + 6 - b, 4), lax.rem(cz + 6 - c, 4)
        return px * 16 + py * 4 + pz

    for group in range(2):
        lanes = slice(128 * group, 128 * (group + 1))
        acc2[...] = jnp.zeros((128, HALF), F32)

        def keys_step(c):
            rows = rows_at(c)
            if group == 0:
                grad_copy(c, 0).wait_recv()
            low = (lgs[rows, lanes].astype(F32) + lgr[rows, lanes].astype(F32)).astype(BF16)
            lg[rows, lanes] = low
            acc2[...] += dot_tn(low, x[rows, :])

        each_chunk(keys_step)
        for q in range(GROUPS6):
            flat[q * 128:(q + 1) * 128, :] = acc2[:, q * 128:(q + 1) * 128].T
        kgmsg[group * 32:(group + 1) * 32, :, :] = flat[0:HALF, :].reshape(32, KROWS, 128).astype(BF16)

        def grad_send(p, group=group):
            return pltpu.make_async_remote_copy(
                kgmsg.at[group * 32 + p], kgland.at[t], a2a_s.at[5], a2a_r.at[5],
                device_id={"tok": g * 32 + p, "grp": group}, device_id_type=MESH,
            )

        def send_grad(i, _):
            grad_send(key_target(i)).start()
            return 0

        def send_near(i, _):
            p = key_target(i)

            @pl.when((g * 32 + p != t) | (g != group))
            def _():
                grad_send(p).start()

            return 0

        lax.fori_loop(0, 20, send_grad, 0, unroll=True)
        lax.fori_loop(22, 32, send_grad, 0, unroll=True)
        lax.fori_loop(20, 22, send_near, 0)

    @pl.when(half == g)
    def _():
        pltpu.make_async_copy(kgmsg.at[g * 32 + lax.rem(t, 32)], kgland.at[t], a2a_r.at[5]).start()

    def tok_step(c):
        rows = rows_at(c)
        value = dot_nn(dispw[rows, :], rval[...]) + dot_nt(lg[rows, :], keyf[...])
        tok_out[rows, :] = value.astype(BF16)

    each_chunk(tok_step)

    landed(5, kgland)
    turned = jnp.sum(kgland[...].astype(F32), axis=0)
    parts = []
    for _ in range(3):
        parts.append(turned.astype(BF16))
        turned = turned - parts[-1].astype(F32)
    key_out[...] = dot_nt(parts[0], order) + (dot_nt(parts[1], order) + dot_nt(parts[2], order))

    for pair in (osg_pair, out_pair):
        pair.wait_send()

    for c in range(NCHUNK):
        logit_copy(c, 0).wait_send()
        logit_copy(c, 1).wait_send()
        grad_copy(c, 0).wait_send()
    sent(1, osgmsg.at[pl.ds(0, NT - 1)])
    sent(2, slotland.at[0])
    sent(2, slotland.at[1, pl.ds(0, NT - 1)])
    sent(3, outland.at[pl.ds(0, NT - 1)])
    sent(4, rtland.at[0])
    sent(4, rtland.at[1, pl.ds(0, NT - 1)])

    @pl.when(half == g)
    def _():
        sent(0, keyland.at[pl.ds(0, NT - 1)])
        sent(5, kgmsg.at[pl.ds(0, NT - 1)])

    @pl.when(half != g)
    def _():
        sent(0, keyland)
        sent(5, kgmsg)


def store(lay, tok, key, win, wout, lay_out, tok_out, key_out, win_out, wout_out, sems):
    pairs = [(key, key_out)]
    for i in range(PIECES):
        rows = pl.ds(i * (TOK // PIECES), TOK // PIECES)
        pairs += [(lay.at[rows], lay_out.at[rows]), (tok.at[rows], tok_out.at[rows])]
        rows = pl.ds(i * (WIDTH // PIECES), WIDTH // PIECES)
        pairs.append((win.at[0, 0, rows], win_out.at[0, 0, rows]))
        rows = pl.ds(i * (HID // PIECES), HID // PIECES)
        pairs.append((wout.at[0, 0, rows], wout_out.at[0, 0, rows]))
    copies = [pltpu.make_async_copy(src, dst, sems.at[i]) for i, (src, dst) in enumerate(pairs)]
    for copy in copies:
        copy.start()
    for copy in copies:
        copy.wait()


def body(tokens, slot_keys, w_in, w_out, out_grad):
    anywhere = pl.BlockSpec(memory_space=pl.ANY)
    vmem = pl.BlockSpec(memory_space=pltpu.VMEM)
    buf = pltpu.VMEM
    dma = pltpu.SemaphoreType.DMA
    paired = buf((2, NT, 16, 128), BF16)
    short = buf((NT, DATA_ROWS, 128), BF16)
    layer_out, tokens_grad, keys_grad, w_in_grad, w_out_grad = pl.pallas_call(
        kernel,
        out_shape=(
            pltpu.VMEM((TOK, HALF), BF16),
            pltpu.VMEM((TOK, HALF), BF16),
            pltpu.VMEM((KROWS, 128), F32),
            pltpu.VMEM(w_in.shape, BF16),
            pltpu.VMEM(w_out.shape, BF16),
        ),
        in_specs=[anywhere] * 5,
        out_specs=[vmem, vmem, vmem, vmem, vmem],
        scratch_shapes=[
            buf((TOK, HALF), BF16),
            buf((TOK, HALF), BF16),
            buf((WIDTH, HID), BF16),
            buf((HID, WIDTH), BF16),
            buf((HID, WIDTH), BF16),
            buf((WIDTH, HID), BF16),
            buf((TOK, SLOTS), F32),
            buf((TOK, SLOTS), F32),
            buf((TOK, SLOTS), F32),
            buf((TOK, SLOTS), BF16),
            buf((TOK, SLOTS), BF16),
            buf((TOK, SLOTS), BF16),
            buf((TOK, SLOTS), BF16),
            buf((TOK, SLOTS), BF16),
            buf((SLOTS, HALF), F32),
            buf((128, HALF), F32),
            buf((2 * NT * 16, 128), F32),
            buf((HALF, SLOTS), BF16),
            buf((KROWS, 128), BF16),
            buf((KROWS, 128), BF16),
            short,
            short,
            short,
            paired,
            paired,
            buf((DATA_ROWS, 128), BF16),
            short,
            buf((2, 16, 128), BF16),
            paired,
            short,
            short,
            buf((SLOTS, HALF), BF16),
            buf((SLOTS, HALF), BF16),
            buf((8, 128), F32),
            buf((8, 128), F32),
            buf((DATA_ROWS, 128), F32),
            buf((SLOTS, HALF), BF16),
            buf((2, 128, HALF), BF16),
            buf((2, 16, 128), F32),
            buf((2, 16, 128), F32),
            buf((2, 16, 128), F32),
            buf((2, 16, 128), F32),
            buf((16, 128), F32),
            buf((16, WIDTH), F32),
            buf((16, WIDTH), F32),
            dma((5,)),
            dma((4,)),
            dma((4,)),
            dma((4,)),
            dma((2, NCHUNK)),
            dma((2, NCHUNK)),
            dma((2, NCHUNK)),
            dma((2, NCHUNK)),
            dma((6,)),
            dma((6,)),
        ],
        compiler_params=pltpu.CompilerParams(
            collective_id=0, has_side_effects=True, vmem_limit_bytes=46 * 1024 * 1024
        ),
        name="moe",
    )(tokens, slot_keys, w_in, w_out, out_grad)
    results = (layer_out, tokens_grad, keys_grad, w_in_grad, w_out_grad)
    results = tuple(pltpu.with_memory_space_constraint(r, pltpu.VMEM) for r in results)
    return pl.pallas_call(
        store,
        out_shape=tuple(jax.ShapeDtypeStruct(r.shape, r.dtype) for r in results),
        in_specs=[vmem] * 5,
        out_specs=[anywhere] * 5,
        scratch_shapes=[dma((4 * PIECES + 1,))],
        compiler_params=pltpu.CompilerParams(has_side_effects=True, vmem_limit_bytes=1024 * 1024),
        name="store",
    )(*results)


def solution(mesh):
    placed = (
        P("tok", "grp"),
        P("tok", "grp"),
        P("grp", "tok", None, None),
        P("grp", "tok", None, None),
        P("tok", "grp"),
    )
    return jax.shard_map(
        body,
        mesh=mesh,
        in_specs=placed,
        out_specs=(
            P("tok", "grp"),
            P("tok", "grp"),
            P("tok", "grp"),
            P("grp", "tok", None, None),
            P("grp", "tok", None, None),
        ),
        check_vma=False,
    )
```
